32 devices in a mesh: groups: 2 (over y), dp: 4 (over x, core), tensor: 4 (over z).
Axes of the slice: x: 2, y: 2, z: 4, core: 2. Of those that a mesh axis runs over, the one named last changes fastest.
Arguments:
- tokens: bfloat16 [4096, 8192], P(('groups', 'dp'), 'tensor'), parts along dimension 0, may hold values from -6 to 6
- cotangent: bfloat16 [4096, 8192], P(('groups', 'dp'), 'tensor'), parts along dimension 0, may hold values from -6 to 6
- segment: int32 [4096], P(('groups', 'dp')), parts along dimension 0, may hold values from 0 to 15, never falling along the last dimension, each value on 1 to 512 neighbouring positions
- owner_slot: int32 [32], P('groups'), parts along dimension 0, may hold values from 0 to 15, each once
- out_weight: bfloat16 [8192, 8192], P(None, 'tensor'), may hold values from -0.0625 to 0.0625
- a_weight: float32 [32, 8192, 64], P(('groups', 'dp'), 'tensor'), parts along dimension 0, may hold values from -0.0625 to 0.0625
- b_weight: float32 [32, 64, 8192], P(('groups', 'dp'), None, 'tensor'), parts along dimension 0, may hold values from -0.75 to 0.75
- a_first: float32 [32, 8192, 64], P(('groups', 'dp'), 'tensor'), parts along dimension 0, may hold values from -1.5 to 1.5
- a_second: float32 [32, 8192, 64], P(('groups', 'dp'), 'tensor'), parts along dimension 0, may hold values from 0.001 to 0.1
- b_first: float32 [32, 64, 8192], P(('groups', 'dp'), None, 'tensor'), parts along dimension 0, may hold values from -0.15 to 0.15
- b_second: float32 [32, 64, 8192], P(('groups', 'dp'), None, 'tensor'), parts along dimension 0, may hold values from 1e-06 to 0.0001
Outputs:
- output: bfloat16 [4096, 8192], P(('groups', 'dp'), 'tensor'), parts along dimension 0
- token_input_gradient: bfloat16 [4096, 8192], P(('groups', 'dp'), 'tensor'), parts along dimension 0
- new_a: float32 [32, 8192, 64], P(('groups', 'dp'), 'tensor'), parts along dimension 0
- new_b: float32 [32, 64, 8192], P(('groups', 'dp'), None, 'tensor'), parts along dimension 0
- new_a_first: float32 [32, 8192, 64], P(('groups', 'dp'), 'tensor'), parts along dimension 0
- new_a_second: float32 [32, 8192, 64], P(('groups', 'dp'), 'tensor'), parts along dimension 0
- new_b_first: float32 [32, 64, 8192], P(('groups', 'dp'), None, 'tensor'), parts along dimension 0
- new_b_second: float32 [32, 64, 8192], P(('groups', 'dp'), None, 'tensor'), parts along dimension 0
The draws below stay inside these ranges and needn't reach their ends.
There are 2 independent parts, one for each index of `groups`. The reference program is written for one: setup_inputs(seed, part) draws one part's arguments, and reference() takes and returns one part's arrays. A program takes and returns all parts, laid end to end along the dimension named above; an argument that names none is the same for every part. Nothing has to cross between parts.
Inputs may be any that keep to these rules, and one draw needn't show every extreme that they name: `segment`: job numbers never fall along the packed tokens; every job has at least one token and some job exactly 512. `owner_slot`: each slot holds exactly one job.
All inputs are finite; a program needn't handle non-finite values.
Results may differ from the reference program's by a relative error of at most 0.0045.
Values may be sent and summed in bfloat16 or wider, within the bound.
A program may use at most 256 MiB of HBM per device.

```python
import math
import jax
import jax.numpy as jnp
import numpy as np
from jax import lax

MODEL_WIDTH = 8192
ADAPTER_RANK = 64
ADJUST_JOBS = 16
TOKENS = 2048


def shard_levels(own_key, extent, pieces, low, top_value):
    def one(axis_at, blocks):
        draws = jax.random.uniform(jax.random.fold_in(jax.random.fold_in(own_key, 6), axis_at), (blocks,), jnp.float32, low / len(pieces), top_value / len(pieces))
        return jnp.repeat(jnp.exp(draws), extent[axis_at] // blocks).reshape((-1,) + (1,) * (len(extent) - axis_at - 1))

    level = one(*pieces[0])
    for cut in pieces[1:]:
        level = level * one(*cut)
    return level


def profile(number_of, total, bound, slope):
    portions = [(1 << 20) // math.isqrt(rank ** slope) + 1 for rank in range(2, number_of + 1)]
    surplus, given = total - bound - (number_of - 1), [1] * (number_of - 1)
    while surplus > 0:
        movable = [i for i in range(number_of - 1) if given[i] < bound]
        pool, budget = sum([portions[i] for i in movable]), surplus
        for i in movable:
            extra = min(bound - given[i], max(1, budget * portions[i] // pool), surplus)
            given[i] = given[i] + extra
            surplus = surplus - extra
    return np.array([bound] + given)


def uneven_parts(stream_key, number_of, total, most, lean):
    if number_of == 2:
        one = jax.random.randint(stream_key, (), max(1, total - most), min(most, total - 1) + 1)
        return jnp.stack([one, total - one])
    lengths = jnp.asarray(profile(number_of, total, most, lean), jnp.int32)
    couples = (number_of - 1) // 2
    donor, taker = lengths[1:1 + 2 * couples:2], lengths[2:2 + 2 * couples:2]
    margin = jnp.minimum(donor - 1, most - taker)
    passed = jax.random.randint(jax.random.fold_in(stream_key, 1), (couples,), 0, 1 << 20) % (margin + 1)
    lengths = lengths.at[1:1 + 2 * couples:2].set(donor - passed).at[2:2 + 2 * couples:2].set(taker + passed)
    return lengths[jax.random.permutation(jax.random.fold_in(stream_key, 2), number_of)]


def centred(stream_key, extent, width, limit, split=(), kind=jnp.bfloat16):
    entries = jax.random.normal(stream_key, extent, jnp.float32) * width
    if len(split) > 0:
        entries = shard_levels(stream_key, extent, split, -0.22, 0.18) * entries
    return jnp.clip(entries, min=-limit, max=limit).astype(kind)


def setup_inputs(seed: int = 0, part: int = 0) -> dict:
    splits = jax.random.split(jax.random.key(seed), 12)
    own_keys = jax.random.split(jax.random.fold_in(splits[11], part), 12)
    return {
        "tokens": centred(own_keys[0], (TOKENS, MODEL_WIDTH), 1.0, 6.0, ((0, 4), (1, 4))),
        "cotangent": centred(own_keys[1], (TOKENS, MODEL_WIDTH), 1.0, 6.0, ((0, 4), (1, 4))),
        "segment": jnp.searchsorted(jnp.cumsum(uneven_parts(own_keys[2], ADJUST_JOBS, TOKENS, TOKENS // 4, 2)), jnp.arange(TOKENS), side="right").astype(jnp.int32),
        "owner_slot": jax.random.permutation(own_keys[3], ADJUST_JOBS).astype(jnp.int32),
        "out_weight": centred(splits[4], (MODEL_WIDTH, MODEL_WIDTH), MODEL_WIDTH ** -0.5, 0.0625, ((1, 4),)),
        "a_weight": centred(own_keys[5], (ADJUST_JOBS, MODEL_WIDTH, ADAPTER_RANK), MODEL_WIDTH ** -0.5, 0.0625, ((0, 4), (1, 4)), jnp.float32),
        "b_weight": centred(own_keys[6], (ADJUST_JOBS, ADAPTER_RANK, MODEL_WIDTH), ADAPTER_RANK ** -0.5, 0.75, ((0, 4), (2, 4)), jnp.float32),
        "a_first": centred(own_keys[7], (ADJUST_JOBS, MODEL_WIDTH, ADAPTER_RANK), 0.25, 1.5, ((0, 4), (1, 4)), jnp.float32),
        "a_second": jnp.clip(jnp.exp(math.log(0.1) - 4.6051702 * jax.random.uniform(own_keys[8], (ADJUST_JOBS, MODEL_WIDTH, ADAPTER_RANK), jnp.float32) ** shard_levels(own_keys[8], (ADJUST_JOBS, MODEL_WIDTH, ADAPTER_RANK), ((0, 4), (1, 4)), -0.2, 0.2)), 0.001, 0.1),
        "b_first": centred(own_keys[9], (ADJUST_JOBS, ADAPTER_RANK, MODEL_WIDTH), 0.025, 0.15, ((0, 4), (2, 4)), jnp.float32),
        "b_second": jnp.clip(jnp.exp(math.log(0.0001) - 4.6051702 * jax.random.uniform(own_keys[10], (ADJUST_JOBS, ADAPTER_RANK, MODEL_WIDTH), jnp.float32) ** shard_levels(own_keys[10], (ADJUST_JOBS, ADAPTER_RANK, MODEL_WIDTH), ((0, 4), (2, 4)), -0.2, 0.2)), 9.999999974752427e-07, 0.0001),
    }


adapter_scale = 0.5
learn_rate = 0.01
beta_first = 0.9
beta_second = 0.999
adam_eps = 1e-08

def adam_step(weight, first, second, grad):
    first_new = beta_first * first + (1.0 - beta_first) * grad
    second_new = beta_second * second + (1.0 - beta_second) * grad * grad
    corr_first = 1.0 - beta_first ** 10
    corr_second = 1.0 - beta_second ** 10
    weight_new = weight - learn_rate * (first_new / corr_first) / (jnp.sqrt(second_new / corr_second) + adam_eps)
    return (weight_new, first_new, second_new)

def reference(tokens, cotangent, segment, owner_slot, out_weight, a_weight, b_weight, a_first, a_second, b_first, b_second):
    job_slot = owner_slot[segment].astype(jnp.int32)
    onehot = (job_slot[:, None] == jnp.arange(ADJUST_JOBS, dtype=jnp.int32)[None, :]).astype(jnp.float32)
    a_half = a_weight.astype(jnp.bfloat16)
    adapter_b_half = b_weight.astype(jnp.bfloat16)
    adapter_a_flat = jnp.transpose(a_half, (1, 0, 2)).reshape(MODEL_WIDTH, ADJUST_JOBS * ADAPTER_RANK)
    b_cols = jnp.transpose(adapter_b_half, (2, 0, 1)).reshape(MODEL_WIDTH, ADJUST_JOBS * ADAPTER_RANK)
    all_down = jnp.dot(tokens, adapter_a_flat, preferred_element_type=jnp.float32).reshape(TOKENS, ADJUST_JOBS, ADAPTER_RANK)
    all_up = jnp.dot(cotangent, b_cols, preferred_element_type=jnp.float32).reshape(TOKENS, ADJUST_JOBS, ADAPTER_RANK)
    down_proj = jnp.einsum('tjk,tj->tk', all_down, onehot)
    up_proj = jnp.einsum('tjk,tj->tk', all_up, onehot)
    down_half = down_proj.astype(jnp.bfloat16)
    up_half = up_proj.astype(jnp.bfloat16)
    down_product_wide = (onehot[:, :, None] * down_half.astype(jnp.float32)[:, None, :]).reshape(TOKENS, ADJUST_JOBS * ADAPTER_RANK).astype(jnp.bfloat16)
    up_product_wide = (onehot[:, :, None] * up_half.astype(jnp.float32)[:, None, :]).reshape(TOKENS, ADJUST_JOBS * ADAPTER_RANK).astype(jnp.bfloat16)
    frozen_output = jnp.dot(tokens, out_weight, preferred_element_type=jnp.float32)
    adapter_output = jnp.dot(down_product_wide, adapter_b_half.reshape(ADJUST_JOBS * ADAPTER_RANK, MODEL_WIDTH), preferred_element_type=jnp.float32)
    output = (frozen_output + adapter_scale * adapter_output).astype(jnp.bfloat16)
    frozen_backward = lax.dot_general(cotangent, out_weight, (((1,), (1,)), ((), ())), preferred_element_type=jnp.float32)
    adapter_backward = lax.dot_general(up_product_wide, adapter_a_flat, (((1,), (1,)), ((), ())), preferred_element_type=jnp.float32)
    token_input_gradient = (frozen_backward + adapter_scale * adapter_backward).astype(jnp.bfloat16)
    token_counts = lax.optimization_barrier(jnp.sum(onehot, axis=0))
    scale_factor = adapter_scale / token_counts
    grad_a = lax.dot_general(tokens, up_product_wide, (((0,), (0,)), ((), ())), preferred_element_type=jnp.float32)
    grad_a = jnp.transpose(grad_a.reshape(MODEL_WIDTH, ADJUST_JOBS, ADAPTER_RANK), (1, 0, 2)) * scale_factor[:, None, None]
    grad_b = lax.dot_general(down_product_wide, cotangent, (((0,), (0,)), ((), ())), preferred_element_type=jnp.float32)
    grad_b = grad_b.reshape(ADJUST_JOBS, ADAPTER_RANK, MODEL_WIDTH) * scale_factor[:, None, None]
    new_a, new_a_first, new_a_second = adam_step(a_weight, a_first, a_second, grad_a)
    new_b, new_b_first, new_b_second = adam_step(b_weight, b_first, b_second, grad_b)
    return (output, token_input_gradient, new_a, new_b, new_a_first, new_a_second, new_b_first, new_b_second)
```

```python
import jax
import jax.numpy as jnp
from jax import lax
from jax.sharding import PartitionSpec as P

adapter_scale = 0.5
learn_rate = 0.01
beta_first = 0.9
beta_second = 0.999
adam_eps = 1e-08


def adam_step(weight, first, second, grad):
    first_new = beta_first * first + (1.0 - beta_first) * grad
    second_new = beta_second * second + (1.0 - beta_second) * grad * grad
    corr_first = 1.0 - beta_first**10
    corr_second = 1.0 - beta_second**10
    weight_new = weight - learn_rate * (first_new / corr_first) / (
        jnp.sqrt(second_new / corr_second) + adam_eps
    )
    return (weight_new, first_new, second_new)


def select_rows(wide, onehot, jobs_all, rank):
    return jnp.einsum("tjk,tj->tk", wide.reshape(wide.shape[0], jobs_all, rank), onehot)


def spread_rows(values, onehot):
    rows = values.shape[0]
    wide = onehot[:, :, None] * values.astype(jnp.float32)[:, None, :]
    return wide.reshape(rows, -1).astype(jnp.bfloat16)


def grouped_sums(tokens, cotangent, out_weight, size):
    me = lax.axis_index("tensor")
    rows, width = tokens.shape
    partial = [
        lax.dot_general(
            cotangent,
            out_weight[at * width : (at + 1) * width],
            (((1,), (1,)), ((), ())),
            preferred_element_type=jnp.float32,
        ).astype(jnp.bfloat16)
        for at in range(size)
    ]
    partial = jnp.stack(partial)
    to_right = [(i, i + 1) for i in range(size - 1)]
    to_left = [(i + 1, i) for i in range(size - 1)]
    from_left, from_right = [], []

    def outgoing(came, turn, place, towards):
        owner = jnp.clip(me + towards * (size - turn), 0, size - 1)
        own = lax.dynamic_index_in_dim(partial, owner, 0, keepdims=False)
        own = jnp.where(turn > place, own.astype(jnp.float32), 0.0)
        return (came.astype(jnp.float32) + own).astype(jnp.bfloat16)

    for turn in range(size):
        if turn == 0:
            right, left = tokens, tokens
        else:
            right = outgoing(from_left[-1], turn, me, 1)
            left = outgoing(from_right[-1], turn, size - 1 - me, -1)
        from_left.append(lax.ppermute(right, "tensor", to_right))
        from_right.append(lax.ppermute(left, "tensor", to_left))

    def rows_of(block):
        return lax.dynamic_slice_in_dim(out_weight, block * width, width, 0)

    frozen = jnp.dot(tokens, rows_of(me), preferred_element_type=jnp.float32)
    lower = me < size // 2
    nearest = jnp.minimum(me, size - 1 - me)
    step = jnp.where(lower, 1, -1)
    for turn in range(size - 1):
        block = jnp.where(lower, from_right[turn], from_left[turn])
        owner = me + step * (turn + 1)
        other = size - 2 - turn
        if turn >= size // 2:
            short = jnp.where(lower, from_left[other], from_right[other])
            use_short = other < nearest
            block = jnp.where(use_short, short, block)
            owner = jnp.where(use_short, me - step * (other + 1), owner)
        frozen = frozen + jnp.dot(block, rows_of(owner), preferred_element_type=jnp.float32)
    own = lax.dynamic_index_in_dim(partial, me, 0, keepdims=False).astype(jnp.float32)
    backward = (
        own + from_left[-1].astype(jnp.float32) + from_right[-1].astype(jnp.float32)
    )
    return frozen, backward


def base_products(tokens, cotangent, out_weight):
    size = lax.axis_size("tensor")
    if size % 2 == 0 and size <= 8:
        return grouped_sums(tokens, cotangent, out_weight, size)
    frozen_output = jnp.dot(
        lax.all_gather(tokens, "tensor", axis=1, tiled=True),
        out_weight,
        preferred_element_type=jnp.float32,
    )
    frozen_backward = lax.psum_scatter(
        lax.dot_general(
            out_weight, cotangent, (((1,), (1,)), ((), ())), preferred_element_type=jnp.float32
        ),
        "tensor",
        scatter_dimension=0,
        tiled=True,
    )
    return frozen_output, jnp.transpose(frozen_backward)


def per_device(
    tokens,
    cotangent,
    segment,
    owner_slot,
    out_weight,
    a_weight,
    b_weight,
    a_first,
    a_second,
    b_first,
    b_second,
):
    local_width = tokens.shape[1]
    rank = a_weight.shape[2]
    jobs_all = owner_slot.shape[0]
    job_slot = owner_slot[segment]
    onehot = (job_slot[:, None] == jnp.arange(jobs_all, dtype=jnp.int32)[None, :]).astype(
        jnp.float32
    )
    a_half = a_weight.astype(jnp.bfloat16)
    adapter_b_half = b_weight.astype(jnp.bfloat16)
    a_every, b_every = (
        lax.all_gather(a_half, "dp", axis=0, tiled=True),
        lax.all_gather(adapter_b_half, "dp", axis=0, tiled=True),
    )
    adapter_a_flat = jnp.transpose(a_every, (1, 0, 2)).reshape(local_width, jobs_all * rank)
    adapter_b_flat = b_every.reshape(jobs_all * rank, local_width)
    down_part = select_rows(
        jnp.dot(tokens, adapter_a_flat, preferred_element_type=jnp.float32), onehot, jobs_all, rank
    )
    up_part = select_rows(
        lax.dot_general(
            cotangent, adapter_b_flat, (((1,), (1,)), ((), ())), preferred_element_type=jnp.float32
        ),
        onehot,
        jobs_all,
        rank,
    )
    down_proj = lax.psum(down_part, "tensor")
    down_product_wide = spread_rows(down_proj.astype(jnp.bfloat16), onehot)
    frozen_output, frozen_backward = base_products(tokens, cotangent, out_weight)
    adapter_output = jnp.dot(down_product_wide, adapter_b_flat, preferred_element_type=jnp.float32)
    output = (frozen_output + adapter_scale * adapter_output).astype(jnp.bfloat16)
    up_proj = lax.psum(up_part, "tensor")
    up_product_wide = spread_rows(up_proj.astype(jnp.bfloat16), onehot)
    adapter_backward = lax.dot_general(
        up_product_wide,
        adapter_a_flat,
        (((1,), (1,)), ((), ())),
        preferred_element_type=jnp.float32,
    )
    token_input_gradient = (frozen_backward + adapter_scale * adapter_backward).astype(jnp.bfloat16)
    grad_a_part = lax.dot_general(
        tokens, up_product_wide, (((0,), (0,)), ((), ())), preferred_element_type=jnp.float32
    )
    grad_a_part = jnp.transpose(grad_a_part.reshape(local_width, jobs_all, rank), (1, 0, 2))
    grad_b_part = lax.dot_general(
        down_product_wide, cotangent, (((0,), (0,)), ((), ())), preferred_element_type=jnp.float32
    )
    grad_b_part = grad_b_part.reshape(jobs_all, rank, local_width)
    count_part = jnp.sum(onehot, axis=0)
    grad_a, grad_b, token_counts = (
        lax.psum_scatter(grad_a_part.astype(jnp.bfloat16), "dp", scatter_dimension=0, tiled=True),
        lax.psum_scatter(grad_b_part.astype(jnp.bfloat16), "dp", scatter_dimension=0, tiled=True),
        lax.psum_scatter(count_part, "dp", scatter_dimension=0, tiled=True),
    )
    scale_factor = adapter_scale / token_counts
    grad_a = grad_a.astype(jnp.float32) * scale_factor[:, None, None]
    grad_b = grad_b.astype(jnp.float32) * scale_factor[:, None, None]
    new_a, new_a_first, new_a_second = adam_step(a_weight, a_first, a_second, grad_a)
    new_b, new_b_first, new_b_second = adam_step(b_weight, b_first, b_second, grad_b)
    return (
        output,
        token_input_gradient,
        new_a,
        new_b,
        new_a_first,
        new_a_second,
        new_b_first,
        new_b_second,
    )


def solution(mesh):
    return jax.shard_map(
        per_device,
        mesh=mesh,
        in_specs=(
            P(("groups", "dp"), "tensor"),
            P(("groups", "dp"), "tensor"),
            P(("groups", "dp")),
            P("groups"),
            P(None, "tensor"),
            P(("groups", "dp"), "tensor", None),
            P(("groups", "dp"), None, "tensor"),
            P(("groups", "dp"), "tensor", None),
            P(("groups", "dp"), "tensor", None),
            P(("groups", "dp"), None, "tensor"),
            P(("groups", "dp"), None, "tensor"),
        ),
        out_specs=(
            P(("groups", "dp"), "tensor"),
            P(("groups", "dp"), "tensor"),
            P(("groups", "dp"), "tensor", None),
            P(("groups", "dp"), None, "tensor"),
            P(("groups", "dp"), "tensor", None),
            P(("groups", "dp"), "tensor", None),
            P(("groups", "dp"), None, "tensor"),
            P(("groups", "dp"), None, "tensor"),
        ),
        check_vma=False,
    )
```

```python
import jax
import jax.numpy as jnp
from jax import lax
from jax.experimental import pallas as pl
from jax.experimental.pallas import tpu as pltpu
from jax.sharding import PartitionSpec as P

adapter_scale = 0.5
learn_rate = 0.01
beta_first = 0.9
beta_second = 0.999
adam_eps = 1e-08


def adam_step(weight, first, second, grad):
    first_new = beta_first * first + (1.0 - beta_first) * grad
    second_new = beta_second * second + (1.0 - beta_second) * grad * grad
    corr_first = 1.0 - beta_first**10
    corr_second = 1.0 - beta_second**10
    weight_new = weight - learn_rate * (first_new / corr_first) / (
        jnp.sqrt(second_new / corr_second) + adam_eps
    )
    return (weight_new, first_new, second_new)


def select_rows(wide, onehot, jobs_all, rank):
    return jnp.einsum("tjk,tj->tk", wide.reshape(wide.shape[0], jobs_all, rank), onehot)


def spread_rows(values, onehot):
    rows = values.shape[0]
    wide = onehot[:, :, None] * values.astype(jnp.float32)[:, None, :]
    return wide.reshape(rows, -1).astype(jnp.bfloat16)


HALVES = 2


def partial_kernel(cotangent, weight, out):
    out[0] = lax.dot_general(
        cotangent[...], weight[...], (((1,), (1,)), ((), ())), preferred_element_type=jnp.float32
    ).astype(out.dtype)


def partial_gradients(cotangent, out_weight, size):
    rows, inner = cotangent.shape
    width = out_weight.shape[0] // size
    tile = min(512, width)
    per_block = width // tile
    return pl.pallas_call(
        partial_kernel,
        grid=(size * per_block,),
        in_specs=[
            pl.BlockSpec((rows, inner), lambda at: (0, 0)),
            pl.BlockSpec((tile, inner), lambda at: (at, 0)),
        ],
        out_specs=pl.BlockSpec((1, rows, tile), lambda at: (at // per_block, 0, at % per_block)),
        out_shape=jax.ShapeDtypeStruct((size, rows, width), jnp.bfloat16),
        compiler_params=pltpu.CompilerParams(vmem_limit_bytes=40 * 1024 * 1024),
        cost_estimate=pl.CostEstimate(
            flops=2 * rows * inner * size * width,
            bytes_accessed=2 * (size * width * inner + rows * inner + rows * size * width),
            transcendentals=0,
        ),
    )(cotangent, out_weight)


def tie(*groups):
    return lax.optimization_barrier(groups)


def line_device(
    tokens,
    cotangent,
    segment,
    owner_slot,
    out_weight,
    a_weight,
    b_weight,
    a_first,
    a_second,
    b_first,
    b_second,
):
    size = lax.axis_size("tensor")
    me = lax.axis_index("tensor")
    rows, width = tokens.shape
    rank = a_weight.shape[2]
    jobs_all = owner_slot.shape[0]
    jobs_own = a_weight.shape[0]
    half_rows = rows // HALVES
    to_right = [(i, i + 1) for i in range(size - 1)]
    to_left = [(i + 1, i) for i in range(size - 1)]

    def exchange(right, left):
        return (
            [lax.ppermute(x, "tensor", to_right) for x in right],
            [lax.ppermute(x, "tensor", to_left) for x in left],
        )

    halves = [tokens[h * half_rows : (h + 1) * half_rows] for h in range(HALVES)]
    from_left, from_right = exchange(halves, halves)
    history = [(from_left, from_right)]

    a_every = lax.all_gather(a_weight.astype(jnp.bfloat16), "dp", axis=0, tiled=True)
    b_every = lax.all_gather(b_weight.astype(jnp.bfloat16), "dp", axis=0, tiled=True)
    jobs = jnp.arange(jobs_all, dtype=jnp.int32)
    by_job = (segment[:, None] == jobs[None, :]).astype(jnp.bfloat16)
    slot_of = (owner_slot[:, None] == jobs[None, :]).astype(jnp.bfloat16)
    onehot = jnp.dot(by_job, slot_of, preferred_element_type=jnp.float32)
    counts_every = lax.all_gather(jnp.sum(onehot, axis=0), "dp", axis=0)
    partial = partial_gradients(cotangent, out_weight, size)

    def outgoing(came, turn, place, towards, h):
        owner = jnp.clip(me + towards * (size - turn), 0, size - 1)
        own = lax.dynamic_slice(partial, (owner, h * half_rows, 0), (1, half_rows, width))[0]
        own = jnp.where(turn > place, own.astype(jnp.float32), 0.0)
        return (came.astype(jnp.float32) + own).astype(jnp.bfloat16)

    def next_round(turn):
        from_left, from_right = history[-1]
        right = [outgoing(from_left[h], turn, me, 1, h) for h in range(HALVES)]
        left = [outgoing(from_right[h], turn, size - 1 - me, -1, h) for h in range(HALVES)]
        history.append(exchange(right, left))
        return right[0]

    def rows_of(block):
        return lax.dynamic_slice_in_dim(out_weight, block * width, width, 0)

    lower = me < size // 2
    nearest = jnp.minimum(me, size - 1 - me)
    step = jnp.where(lower, 1, -1)

    def joined(pair, choose):
        return jnp.concatenate(
            [jnp.where(choose, r, l) for l, r in zip(pair[0], pair[1])], axis=0
        )

    def add_block(frozen, turn):
        block = joined(history[turn], lower)
        owner = me + step * (turn + 1)
        other = size - 2 - turn
        if turn >= size // 2:
            short = joined(history[other], jnp.logical_not(lower))
            use_short = other < nearest
            block = jnp.where(use_short, short, block)
            owner = jnp.where(use_short, me - step * (other + 1), owner)
        return frozen + jnp.dot(block, rows_of(owner), preferred_element_type=jnp.float32)

    (history[0], partial, a_every, b_every) = tie(history[0], partial, a_every, b_every)
    mark = next_round(1)
    (mark, a_every, b_every) = tie(mark, a_every, b_every)
    adapter_a_flat = jnp.transpose(a_every, (1, 0, 2)).reshape(width, jobs_all * rank)
    adapter_b_flat = b_every.reshape(jobs_all * rank, width)
    down_part = select_rows(
        jnp.dot(tokens, adapter_a_flat, preferred_element_type=jnp.float32), onehot, jobs_all, rank
    )
    up_part = select_rows(
        lax.dot_general(
            cotangent, adapter_b_flat, (((1,), (1,)), ((), ())), preferred_element_type=jnp.float32
        ),
        onehot,
        jobs_all,
        rank,
    )
    both_every = lax.all_gather(jnp.concatenate([down_part, up_part], axis=1), "tensor", axis=0)
    frozen = jnp.dot(tokens, rows_of(me), preferred_element_type=jnp.float32)
    frozen = add_block(frozen, 0)
    (history[1], frozen, both_every) = tie(history[1], frozen, both_every)

    mark = next_round(2)
    (mark, both_every) = tie(mark, both_every)
    both_half = jnp.sum(both_every, axis=0).astype(jnp.bfloat16)
    down_product_wide = spread_rows(both_half[:, :rank], onehot)
    up_product_wide = spread_rows(both_half[:, rank:], onehot)
    grad_a_part = lax.dot_general(
        tokens, up_product_wide, (((0,), (0,)), ((), ())), preferred_element_type=jnp.float32
    ).astype(jnp.bfloat16)
    grad_a_part = jnp.transpose(grad_a_part.reshape(width, jobs_all, rank), (1, 0, 2))
    grad_b_part = lax.dot_general(
        down_product_wide, cotangent, (((0,), (0,)), ((), ())), preferred_element_type=jnp.float32
    ).astype(jnp.bfloat16)
    grad_b_part = grad_b_part.reshape(jobs_all, rank, width)
    grad_a = lax.psum_scatter(grad_a_part, "dp", scatter_dimension=0, tiled=True)
    grad_b = lax.psum_scatter(grad_b_part, "dp", scatter_dimension=0, tiled=True)
    for turn in range(1, size - 2):
        frozen = add_block(frozen, turn)
    for turn in range(2, size - 1):
        (history[turn], frozen) = tie(history[turn], frozen)
        next_round(turn + 1)

    frozen = add_block(frozen, size - 2)
    adapter_output = jnp.dot(down_product_wide, adapter_b_flat, preferred_element_type=jnp.float32)
    output = (frozen + adapter_scale * adapter_output).astype(jnp.bfloat16)
    adapter_backward = lax.dot_general(
        up_product_wide,
        adapter_a_flat,
        (((1,), (1,)), ((), ())),
        preferred_element_type=jnp.float32,
    )
    own = lax.dynamic_index_in_dim(partial, me, 0, keepdims=False).astype(jnp.float32)
    backward = own + adapter_scale * adapter_backward
    data = lax.axis_index("dp")
    counts = lax.dynamic_slice_in_dim(jnp.sum(counts_every, axis=0), data * jobs_own, jobs_own)
    scale_factor = adapter_scale / counts
    grad_a = grad_a.astype(jnp.float32) * scale_factor[:, None, None]
    grad_b = grad_b.astype(jnp.float32) * scale_factor[:, None, None]
    updated_a = adam_step(a_weight, a_first, a_second, grad_a)
    updated_b = adam_step(b_weight, b_first, b_second, grad_b)
    (history[-1], output, backward, updated_a, updated_b) = tie(
        history[-1], output, backward, updated_a, updated_b
    )
    from_left, from_right = history[-1]
    token_input_gradient = jnp.concatenate(
        [
            (
                backward[h * half_rows : (h + 1) * half_rows]
                + from_left[h].astype(jnp.float32)
                + from_right[h].astype(jnp.float32)
            ).astype(jnp.bfloat16)
            for h in range(HALVES)
        ],
        axis=0,
    )
    new_a, new_a_first, new_a_second = updated_a
    new_b, new_b_first, new_b_second = updated_b
    return (
        output,
        token_input_gradient,
        new_a,
        new_b,
        new_a_first,
        new_a_second,
        new_b_first,
        new_b_second,
    )


def long_device(
    tokens,
    cotangent,
    segment,
    owner_slot,
    out_weight,
    a_weight,
    b_weight,
    a_first,
    a_second,
    b_first,
    b_second,
):
    local_width = tokens.shape[1]
    rank = a_weight.shape[2]
    jobs_all = owner_slot.shape[0]
    job_slot = owner_slot[segment]
    onehot = (job_slot[:, None] == jnp.arange(jobs_all, dtype=jnp.int32)[None, :]).astype(
        jnp.float32
    )
    a_half = a_weight.astype(jnp.bfloat16)
    adapter_b_half = b_weight.astype(jnp.bfloat16)
    a_every, b_every = (
        lax.all_gather(a_half, "dp", axis=0, tiled=True),
        lax.all_gather(adapter_b_half, "dp", axis=0, tiled=True),
    )
    adapter_a_flat = jnp.transpose(a_every, (1, 0, 2)).reshape(local_width, jobs_all * rank)
    adapter_b_flat = b_every.reshape(jobs_all * rank, local_width)
    down_part = select_rows(
        jnp.dot(tokens, adapter_a_flat, preferred_element_type=jnp.float32), onehot, jobs_all, rank
    )
    up_part = select_rows(
        lax.dot_general(
            cotangent, adapter_b_flat, (((1,), (1,)), ((), ())), preferred_element_type=jnp.float32
        ),
        onehot,
        jobs_all,
        rank,
    )
    down_proj = lax.psum(down_part, "tensor")
    down_product_wide = spread_rows(down_proj.astype(jnp.bfloat16), onehot)
    weight_rows = out_weight
    frozen_output = jnp.dot(
        lax.all_gather(tokens, "tensor", axis=1, tiled=True),
        weight_rows,
        preferred_element_type=jnp.float32,
    )
    adapter_output = jnp.dot(down_product_wide, adapter_b_flat, preferred_element_type=jnp.float32)
    output = (frozen_output + adapter_scale * adapter_output).astype(jnp.bfloat16)
    up_proj = lax.psum(up_part, "tensor")
    up_product_wide = spread_rows(up_proj.astype(jnp.bfloat16), onehot)
    weight_rows = out_weight
    frozen_backward = jnp.transpose(
        lax.psum_scatter(
            lax.dot_general(
                weight_rows, cotangent, (((1,), (1,)), ((), ())), preferred_element_type=jnp.float32
            ),
            "tensor",
            scatter_dimension=0,
            tiled=True,
        )
    )
    adapter_backward = lax.dot_general(
        up_product_wide,
        adapter_a_flat,
        (((1,), (1,)), ((), ())),
        preferred_element_type=jnp.float32,
    )
    token_input_gradient = (frozen_backward + adapter_scale * adapter_backward).astype(jnp.bfloat16)
    grad_a_part = lax.dot_general(
        tokens, up_product_wide, (((0,), (0,)), ((), ())), preferred_element_type=jnp.float32
    )
    grad_a_part = jnp.transpose(grad_a_part.reshape(local_width, jobs_all, rank), (1, 0, 2))
    grad_b_part = lax.dot_general(
        down_product_wide, cotangent, (((0,), (0,)), ((), ())), preferred_element_type=jnp.float32
    )
    grad_b_part = grad_b_part.reshape(jobs_all, rank, local_width)
    count_part = jnp.sum(onehot, axis=0)
    grad_a, grad_b, token_counts = (
        lax.psum_scatter(grad_a_part, "dp", scatter_dimension=0, tiled=True),
        lax.psum_scatter(grad_b_part, "dp", scatter_dimension=0, tiled=True),
        lax.psum_scatter(count_part, "dp", scatter_dimension=0, tiled=True),
    )
    scale_factor = adapter_scale / token_counts
    grad_a = grad_a * scale_factor[:, None, None]
    grad_b = grad_b * scale_factor[:, None, None]
    new_a, new_a_first, new_a_second = adam_step(a_weight, a_first, a_second, grad_a)
    new_b, new_b_first, new_b_second = adam_step(b_weight, b_first, b_second, grad_b)
    return (
        output,
        token_input_gradient,
        new_a,
        new_b,
        new_a_first,
        new_a_second,
        new_b_first,
        new_b_second,
    )


def per_device(*arrays):
    size = lax.axis_size("tensor")
    if size % 2 == 0 and 4 <= size <= 8:
        return line_device(*arrays)
    return long_device(*arrays)


def solution(mesh):
    return jax.shard_map(
        per_device,
        mesh=mesh,
        in_specs=(
            P(("groups", "dp"), "tensor"),
            P(("groups", "dp"), "tensor"),
            P(("groups", "dp")),
            P("groups"),
            P(None, "tensor"),
            P(("groups", "dp"), "tensor", None),
            P(("groups", "dp"), None, "tensor"),
            P(("groups", "dp"), "tensor", None),
            P(("groups", "dp"), "tensor", None),
            P(("groups", "dp"), None, "tensor"),
            P(("groups", "dp"), None, "tensor"),
        ),
        out_specs=(
            P(("groups", "dp"), "tensor"),
            P(("groups", "dp"), "tensor"),
            P(("groups", "dp"), "tensor", None),
            P(("groups", "dp"), None, "tensor"),
            P(("groups", "dp"), "tensor", None),
            P(("groups", "dp"), "tensor", None),
            P(("groups", "dp"), None, "tensor"),
            P(("groups", "dp"), None, "tensor"),
        ),
        check_vma=False,
    )
```

```python
import jax
import jax.numpy as jnp
from jax import lax
from jax.sharding import PartitionSpec as P

adapter_scale = 0.5
learn_rate = 0.01
beta_first = 0.9
beta_second = 0.999
adam_eps = 1e-08


def adam_step(weight, first, second, grad):
    first_new = beta_first * first + (1.0 - beta_first) * grad
    second_new = beta_second * second + (1.0 - beta_second) * grad * grad
    corr_first = 1.0 - beta_first**10
    corr_second = 1.0 - beta_second**10
    weight_new = weight - learn_rate * (first_new / corr_first) / (
        jnp.sqrt(second_new / corr_second) + adam_eps
    )
    return (weight_new, first_new, second_new)


def select_rows(wide, onehot, jobs_all, rank):
    return jnp.einsum("tjk,tj->tk", wide.reshape(wide.shape[0], jobs_all, rank), onehot)


def spread_rows(values, onehot):
    rows = values.shape[0]
    wide = onehot[:, :, None] * values.astype(jnp.float32)[:, None, :]
    return wide.reshape(rows, -1).astype(jnp.bfloat16)


HALVES = 2


def partial_gradients(cotangent, out_weight):
    return lax.dot_general(
        cotangent, out_weight, (((1,), (1,)), ((), ())), preferred_element_type=jnp.float32
    ).astype(jnp.bfloat16)


def tie(*groups):
    return lax.optimization_barrier(groups)


def line_device(
    tokens,
    cotangent,
    segment,
    owner_slot,
    out_weight,
    a_weight,
    b_weight,
    a_first,
    a_second,
    b_first,
    b_second,
):
    size = lax.axis_size("tensor")
    me = lax.axis_index("tensor")
    rows, width = tokens.shape
    rank = a_weight.shape[2]
    jobs_all = owner_slot.shape[0]
    jobs_own = a_weight.shape[0]
    half_rows = rows // HALVES
    to_right = [(i, i + 1) for i in range(size - 1)]
    to_left = [(i + 1, i) for i in range(size - 1)]

    def exchange(right, left):
        return (
            [lax.ppermute(x, "tensor", to_right) for x in right],
            [lax.ppermute(x, "tensor", to_left) for x in left],
        )

    halves = [tokens[h * half_rows : (h + 1) * half_rows] for h in range(HALVES)]
    from_left, from_right = exchange(halves, halves)
    history = [(from_left, from_right)]

    a_every = lax.all_gather(a_weight.astype(jnp.bfloat16), "dp", axis=0, tiled=True)
    b_every = lax.all_gather(b_weight.astype(jnp.bfloat16), "dp", axis=0, tiled=True)
    jobs = jnp.arange(jobs_all, dtype=jnp.int32)
    by_job = (segment[:, None] == jobs[None, :]).astype(jnp.bfloat16)
    slot_of = (owner_slot[:, None] == jobs[None, :]).astype(jnp.bfloat16)
    onehot = jnp.dot(by_job, slot_of, preferred_element_type=jnp.float32)
    counts_every = lax.all_gather(jnp.sum(onehot, axis=0), "dp", axis=0)
    partial = partial_gradients(cotangent, out_weight)

    def outgoing(came, turn, place, towards, h):
        owner = jnp.clip(me + towards * (size - turn), 0, size - 1)
        own = lax.dynamic_slice(partial, (h * half_rows, owner * width), (half_rows, width))
        own = jnp.where(turn > place, own.astype(jnp.float32), 0.0)
        return (came.astype(jnp.float32) + own).astype(jnp.bfloat16)

    def next_round(turn):
        from_left, from_right = history[-1]
        right = [outgoing(from_left[h], turn, me, 1, h) for h in range(HALVES)]
        left = [outgoing(from_right[h], turn, size - 1 - me, -1, h) for h in range(HALVES)]
        history.append(exchange(right, left))
        return right[0]

    def rows_of(block):
        return lax.dynamic_slice_in_dim(out_weight, block * width, width, 0)

    lower = me < size // 2
    nearest = jnp.minimum(me, size - 1 - me)
    step = jnp.where(lower, 1, -1)

    def joined(pair, choose):
        return jnp.concatenate(
            [jnp.where(choose, r, l) for l, r in zip(pair[0], pair[1])], axis=0
        )

    def add_block(frozen, turn):
        block = joined(history[turn], lower)
        owner = me + step * (turn + 1)
        other = size - 2 - turn
        if turn >= size // 2:
            short = joined(history[other], jnp.logical_not(lower))
            use_short = other < nearest
            block = jnp.where(use_short, short, block)
            owner = jnp.where(use_short, me - step * (other + 1), owner)
        return frozen + jnp.dot(block, rows_of(owner), preferred_element_type=jnp.float32)

    (history[0], partial, counts_every) = tie(history[0], partial, counts_every)
    mark = next_round(1)
    (mark, a_every, b_every) = tie(mark, a_every, b_every)
    adapter_a_flat = jnp.transpose(a_every, (1, 0, 2)).reshape(width, jobs_all * rank)
    adapter_b_flat = b_every.reshape(jobs_all * rank, width)
    down_part = select_rows(
        jnp.dot(tokens, adapter_a_flat, preferred_element_type=jnp.float32), onehot, jobs_all, rank
    )
    up_part = select_rows(
        lax.dot_general(
            cotangent, adapter_b_flat, (((1,), (1,)), ((), ())), preferred_element_type=jnp.float32
        ),
        onehot,
        jobs_all,
        rank,
    )
    both_every = lax.all_gather(jnp.concatenate([down_part, up_part], axis=1), "tensor", axis=0)
    frozen = jnp.dot(tokens, rows_of(me), preferred_element_type=jnp.float32)
    frozen = add_block(frozen, 0)
    both_half = jnp.sum(both_every, axis=0).astype(jnp.bfloat16)
    down_product_wide = spread_rows(both_half[:, :rank], onehot)
    up_product_wide = spread_rows(both_half[:, rank:], onehot)
    grad_a_part = lax.dot_general(
        tokens, up_product_wide, (((0,), (0,)), ((), ())), preferred_element_type=jnp.float32
    ).astype(jnp.bfloat16)
    grad_a_part = jnp.transpose(grad_a_part.reshape(width, jobs_all, rank), (1, 0, 2))
    grad_b_part = lax.dot_general(
        down_product_wide, cotangent, (((0,), (0,)), ((), ())), preferred_element_type=jnp.float32
    ).astype(jnp.bfloat16)
    grad_b_part = grad_b_part.reshape(jobs_all, rank, width)
    (history[1], frozen, grad_a_part, grad_b_part) = tie(
        history[1], frozen, grad_a_part, grad_b_part
    )

    next_round(2)
    grad_a = lax.psum_scatter(grad_a_part, "dp", scatter_dimension=0, tiled=True)
    grad_b = lax.psum_scatter(grad_b_part, "dp", scatter_dimension=0, tiled=True)
    for turn in range(1, size - 2):
        frozen = add_block(frozen, turn)
    for turn in range(2, size - 1):
        (history[turn], frozen) = tie(history[turn], frozen)
        next_round(turn + 1)

    frozen = add_block(frozen, size - 2)
    adapter_output = jnp.dot(down_product_wide, adapter_b_flat, preferred_element_type=jnp.float32)
    output = (frozen + adapter_scale * adapter_output).astype(jnp.bfloat16)
    adapter_backward = lax.dot_general(
        up_product_wide,
        adapter_a_flat,
        (((1,), (1,)), ((), ())),
        preferred_element_type=jnp.float32,
    )
    own = lax.dynamic_slice_in_dim(partial, me * width, width, 1).astype(jnp.float32)
    backward = own + adapter_scale * adapter_backward
    data = lax.axis_index("dp")
    counts = lax.dynamic_slice_in_dim(jnp.sum(counts_every, axis=0), data * jobs_own, jobs_own)
    scale_factor = adapter_scale / counts
    grad_a = grad_a.astype(jnp.float32) * scale_factor[:, None, None]
    grad_b = grad_b.astype(jnp.float32) * scale_factor[:, None, None]
    updated_a = adam_step(a_weight, a_first, a_second, grad_a)
    updated_b = adam_step(b_weight, b_first, b_second, grad_b)
    (history[-1], output, backward, updated_a, updated_b) = tie(
        history[-1], output, backward, updated_a, updated_b
    )
    from_left, from_right = history[-1]
    token_input_gradient = jnp.concatenate(
        [
            (
                backward[h * half_rows : (h + 1) * half_rows]
                + from_left[h].astype(jnp.float32)
                + from_right[h].astype(jnp.float32)
            ).astype(jnp.bfloat16)
            for h in range(HALVES)
        ],
        axis=0,
    )
    new_a, new_a_first, new_a_second = updated_a
    new_b, new_b_first, new_b_second = updated_b
    return (
        output,
        token_input_gradient,
        new_a,
        new_b,
        new_a_first,
        new_a_second,
        new_b_first,
        new_b_second,
    )


def long_device(
    tokens,
    cotangent,
    segment,
    owner_slot,
    out_weight,
    a_weight,
    b_weight,
    a_first,
    a_second,
    b_first,
    b_second,
):
    local_width = tokens.shape[1]
    rank = a_weight.shape[2]
    jobs_all = owner_slot.shape[0]
    job_slot = owner_slot[segment]
    onehot = (job_slot[:, None] == jnp.arange(jobs_all, dtype=jnp.int32)[None, :]).astype(
        jnp.float32
    )
    a_half = a_weight.astype(jnp.bfloat16)
    adapter_b_half = b_weight.astype(jnp.bfloat16)
    a_every, b_every = (
        lax.all_gather(a_half, "dp", axis=0, tiled=True),
        lax.all_gather(adapter_b_half, "dp", axis=0, tiled=True),
    )
    adapter_a_flat = jnp.transpose(a_every, (1, 0, 2)).reshape(local_width, jobs_all * rank)
    adapter_b_flat = b_every.reshape(jobs_all * rank, local_width)
    down_part = select_rows(
        jnp.dot(tokens, adapter_a_flat, preferred_element_type=jnp.float32), onehot, jobs_all, rank
    )
    up_part = select_rows(
        lax.dot_general(
            cotangent, adapter_b_flat, (((1,), (1,)), ((), ())), preferred_element_type=jnp.float32
        ),
        onehot,
        jobs_all,
        rank,
    )
    down_proj = lax.psum(down_part, "tensor")
    down_product_wide = spread_rows(down_proj.astype(jnp.bfloat16), onehot)
    weight_rows = out_weight
    frozen_output = jnp.dot(
        lax.all_gather(tokens, "tensor", axis=1, tiled=True),
        weight_rows,
        preferred_element_type=jnp.float32,
    )
    adapter_output = jnp.dot(down_product_wide, adapter_b_flat, preferred_element_type=jnp.float32)
    output = (frozen_output + adapter_scale * adapter_output).astype(jnp.bfloat16)
    up_proj = lax.psum(up_part, "tensor")
    up_product_wide = spread_rows(up_proj.astype(jnp.bfloat16), onehot)
    weight_rows = out_weight
    frozen_backward = jnp.transpose(
        lax.psum_scatter(
            lax.dot_general(
                weight_rows, cotangent, (((1,), (1,)), ((), ())), preferred_element_type=jnp.float32
            ),
            "tensor",
            scatter_dimension=0,
            tiled=True,
        )
    )
    adapter_backward = lax.dot_general(
        up_product_wide,
        adapter_a_flat,
        (((1,), (1,)), ((), ())),
        preferred_element_type=jnp.float32,
    )
    token_input_gradient = (frozen_backward + adapter_scale * adapter_backward).astype(jnp.bfloat16)
    grad_a_part = lax.dot_general(
        tokens, up_product_wide, (((0,), (0,)), ((), ())), preferred_element_type=jnp.float32
    )
    grad_a_part = jnp.transpose(grad_a_part.reshape(local_width, jobs_all, rank), (1, 0, 2))
    grad_b_part = lax.dot_general(
        down_product_wide, cotangent, (((0,), (0,)), ((), ())), preferred_element_type=jnp.float32
    )
    grad_b_part = grad_b_part.reshape(jobs_all, rank, local_width)
    count_part = jnp.sum(onehot, axis=0)
    grad_a, grad_b, token_counts = (
        lax.psum_scatter(grad_a_part, "dp", scatter_dimension=0, tiled=True),
        lax.psum_scatter(grad_b_part, "dp", scatter_dimension=0, tiled=True),
        lax.psum_scatter(count_part, "dp", scatter_dimension=0, tiled=True),
    )
    scale_factor = adapter_scale / token_counts
    grad_a = grad_a * scale_factor[:, None, None]
    grad_b = grad_b * scale_factor[:, None, None]
    new_a, new_a_first, new_a_second = adam_step(a_weight, a_first, a_second, grad_a)
    new_b, new_b_first, new_b_second = adam_step(b_weight, b_first, b_second, grad_b)
    return (
        output,
        token_input_gradient,
        new_a,
        new_b,
        new_a_first,
        new_a_second,
        new_b_first,
        new_b_second,
    )


def per_device(*arrays):
    size = lax.axis_size("tensor")
    if size % 2 == 0 and 4 <= size <= 8:
        return line_device(*arrays)
    return long_device(*arrays)


def solution(mesh):
    return jax.shard_map(
        per_device,
        mesh=mesh,
        in_specs=(
            P(("groups", "dp"), "tensor"),
            P(("groups", "dp"), "tensor"),
            P(("groups", "dp")),
            P("groups"),
            P(None, "tensor"),
            P(("groups", "dp"), "tensor", None),
            P(("groups", "dp"), None, "tensor"),
            P(("groups", "dp"), "tensor", None),
            P(("groups", "dp"), "tensor", None),
            P(("groups", "dp"), None, "tensor"),
            P(("groups", "dp"), None, "tensor"),
        ),
        out_specs=(
            P(("groups", "dp"), "tensor"),
            P(("groups", "dp"), "tensor"),
            P(("groups", "dp"), "tensor", None),
            P(("groups", "dp"), None, "tensor"),
            P(("groups", "dp"), "tensor", None),
            P(("groups", "dp"), "tensor", None),
            P(("groups", "dp"), None, "tensor"),
            P(("groups", "dp"), None, "tensor"),
        ),
        check_vma=False,
    )
```
